128 devices in a mesh: expert: 16 (over y, x), replica: 8 (over z, core).
Axes of the slice: x: 4, y: 4, z: 4, core: 2. Of those that a mesh axis runs over, the one named last changes fastest.
Arguments:
- tokens: bfloat16 [16384, 2048], P(('expert', 'replica')), may hold values from -6 to 6
- cotangent: bfloat16 [16384, 2048], P(('expert', 'replica')), may hold values from -0.59765625 to 0.59765625
- gates: bfloat16 [16384, 8], P(('expert', 'replica')), may hold values from 0.019897461 to 0.29882812
- routes: int32 [16384, 8], P(('expert', 'replica')), may hold values from 0 to 31, all different within a row; in each aligned block of 128 rows (0 to 127, 128 to 255, ...) at most 48 rows name the same one
- w_gate: bfloat16 [32, 2048, 512], P('expert'), may hold values from -0.125 to 0.125
- w_up: bfloat16 [32, 2048, 512], P('expert'), may hold values from -0.125 to 0.125
- w_down: bfloat16 [32, 512, 2048], P('expert'), may hold values from -0.25 to 0.25
Outputs:
- grad_input: bfloat16 [16384, 2048], P(('expert', 'replica'))
- grad_gates: bfloat16 [16384, 8], P(('expert', 'replica'))
- grad_w_gate: bfloat16 [32, 2048, 512], P('expert', 'replica')
- grad_w_up: bfloat16 [32, 2048, 512], P('expert', 'replica')
- grad_w_down: bfloat16 [32, 512, 2048], P('expert', None, 'replica')
The draws below stay inside these ranges and needn't reach their ends.
Inputs may be any that keep to these rules, and one draw needn't show every extreme that they name: Among the rows of one device (aligned blocks of 128 tokens), no expert is named by more than 48 routes, and in every draw some expert is named by exactly 48 routes of one device. The 8 experts of a token differ.
All inputs are finite; a program needn't handle non-finite values.
Results may differ from the reference program's by a relative error of at most 0.017.
Values may be sent and summed in bfloat16 or wider, within the bound.
No kernel may reach another device: no remote copies, remote signals or barrier semaphores. Data moves between devices by JAX's collectives and lax.ppermute only.
A program may use at most 128 MiB of HBM per device.

```python
import math
import jax
import jax.numpy as jnp
import numpy as np
from jax import lax

D = 2048
FF = 512
TOP = 8
TOK_DEV = 128
EXPERTS = 32
MOST = 48
TOKENS = 16384
N_EXPERT = 16
N_REPLICA = 8


def levels(rng, dims, split, low, high):
    def one(axis_at, shards_of):
        draws = jax.random.uniform(jax.random.fold_in(jax.random.fold_in(rng, 6), axis_at), (shards_of,), jnp.float32, low / len(split), high / len(split))
        return jnp.repeat(jnp.exp(draws), dims[axis_at] // shards_of).reshape((-1,) + (1,) * (len(dims) - axis_at - 1))

    loudness = one(*split[0])
    for cut in split[1:]:
        loudness = loudness * one(*cut)
    return loudness


def shared_out(own_key, own, number, rows, count, top, most, slope):
    sequence = jax.random.permutation(own_key, count)
    crowded, usual = load_shares(count, rows * top, most, slope, True), load_shares(count, rows * top, most, slope, False)
    places = jnp.arange(count)

    def named(tallies, turn):
        used = int((tallies > 0).sum())
        fixed = max(1, used // 4)
        shifted = fixed + (places - fixed + turn * (used - fixed)) % max(1, count - fixed)
        return jnp.zeros((count,), jnp.int32).at[sequence[jnp.where(places < fixed, places, shifted)]].set(jnp.asarray(tallies, jnp.int32))

    tallies = jnp.where(number % 4 == 0, named(crowded, number // 4), named(usual, number - number // 4 - 1))
    mixed = jax.random.permutation(jax.random.fold_in(own, 3), count)
    giver, receiver = mixed[0:count // 2 * 2:2], mixed[1:count // 2 * 2:2]
    margin = jnp.minimum(tallies[giver] - 1, most - tallies[receiver]) // 2
    margin = jnp.where((giver == sequence[0]) | (receiver == sequence[0]) | (tallies[receiver] == 0), 0, jnp.maximum(margin, 0))
    shifted = jax.random.randint(jax.random.fold_in(own, 4), (count // 2,), 0, 1 << 20) % (margin + 1)
    tallies = tallies.at[giver].add(-shifted).at[receiver].add(shifted)
    labels = jnp.searchsorted(jnp.cumsum(tallies), jnp.arange(rows * top), side="right").astype(jnp.int32)
    listing = labels.reshape(top, rows).T
    listing = listing[jax.random.permutation(jax.random.fold_in(own, 1), rows)]
    turn = jax.random.randint(jax.random.fold_in(own, 2), (rows, 1), 0, top)
    return jnp.take_along_axis(listing, (jnp.arange(top)[None, :] + turn) % top, axis=1)


def load_shares(count, total, reach, lean, full):
    portions = [(1 << 20) // math.isqrt(grade ** lean) + 1 for grade in range(1, count + 1)]
    largest = reach if full else min(reach, max(-(-total // count), total * portions[0] // sum(portions)))
    least = 1 if total - largest >= count - 1 else 0
    given, spare = [largest] + [least] * (count - 1), total - largest - least * (count - 1)
    while spare > 0:
        candidates = [i for i in range(1, count) if given[i] < largest] or [i for i in range(1, count) if given[i] < reach]
        whole, remaining = sum([portions[i] for i in candidates]), spare
        for i in candidates:
            addition = min(reach - given[i], max(1, remaining * portions[i] // whole), spare)
            given[i] = given[i] + addition
            spare = spare - addition
    return np.array(given)


def bell_draw(rng, extent, width, limit, split=(), kind=jnp.bfloat16):
    level = levels(rng, extent, split, -0.22, 0.18) if split else 1.0
    values = jax.random.normal(rng, extent, jnp.float32) * width * level
    return jnp.minimum(jnp.maximum(values, -limit), limit).astype(kind)


def setup_inputs(seed: int = 0) -> dict:
    keys = jax.random.split(jax.random.key(seed), 8)
    tokens = bell_draw(keys[0], (TOKENS, D), 1.0, 6.0, ((0, 128),))
    cotangent = bell_draw(keys[1], (TOKENS, D), 0.1, 0.59765625, ((0, 128),))
    gates = jnp.clip(0.019897461 + 0.27893066 * jax.random.uniform(keys[2], (TOKENS, TOP), jnp.float32) ** levels(keys[2], (TOKENS, TOP), ((0, 128),), -0.2, 0.2), 0.019897461, 0.29882812).astype(jnp.bfloat16)
    routes_keys = jax.random.split(jax.random.fold_in(keys[3], 1), TOKENS // TOK_DEV)
    routes_turns = jax.random.permutation(jax.random.fold_in(keys[3], 3), TOKENS // TOK_DEV)
    routes = jax.vmap(lambda own, number: shared_out(jax.random.fold_in(keys[3], 2), own, number, TOK_DEV, EXPERTS, TOP, MOST, 2))(routes_keys, routes_turns).reshape((TOKENS, TOP))
    w_gate = bell_draw(keys[4], (EXPERTS, D, FF), D ** -0.5, 0.125, ((0, 16),))
    w_up = bell_draw(keys[5], (EXPERTS, D, FF), D ** -0.5, 0.125, ((0, 16),))
    w_down = bell_draw(keys[6], (EXPERTS, FF, D), FF ** -0.5, 0.25, ((0, 16),))
    return {"tokens": tokens, "cotangent": cotangent, "gates": gates, "routes": routes, "w_gate": w_gate, "w_up": w_up, "w_down": w_down}


def first_phase(inputs, upstream, weights_row, gate_matrix, up_matrix, down_matrix):
    gate_pre = jnp.dot(inputs, gate_matrix, preferred_element_type=jnp.float32)
    up_pre = jnp.dot(inputs, up_matrix, preferred_element_type=jnp.float32)
    sigmoid_gate = jax.nn.sigmoid(gate_pre)
    activated = gate_pre * sigmoid_gate
    hidden = (activated * up_pre).astype(jnp.bfloat16)
    expert_out = jnp.dot(hidden, down_matrix, preferred_element_type=jnp.float32)
    gate_grad = jnp.sum(upstream.astype(jnp.float32) * expert_out, axis=1).astype(jnp.bfloat16)
    scaled = (weights_row.astype(jnp.float32)[:, None] * upstream.astype(jnp.float32)).astype(jnp.bfloat16)
    down_grad = lax.dot_general(hidden, scaled, (((0,), (0,)), ((), ())), preferred_element_type=jnp.float32)
    return gate_pre, up_pre, sigmoid_gate, activated, scaled, gate_grad, down_grad


def second_phase(inputs, gate_pre, up_pre, sigmoid_gate, activated, scaled, gate_matrix, up_matrix, down_matrix):
    hidden_grad = lax.dot_general(scaled, down_matrix, (((1,), (1,)), ((), ())), preferred_element_type=jnp.float32)
    pre_gate_grad = (hidden_grad * up_pre * sigmoid_gate * (1.0 + gate_pre * (1.0 - sigmoid_gate))).astype(jnp.bfloat16)
    pre_up_grad = (hidden_grad * activated).astype(jnp.bfloat16)
    input_grad = lax.dot_general(pre_gate_grad, gate_matrix, (((1,), (1,)), ((), ())), preferred_element_type=jnp.float32)
    input_grad = input_grad + lax.dot_general(pre_up_grad, up_matrix, (((1,), (1,)), ((), ())), preferred_element_type=jnp.float32)
    gate_weight_grad = lax.dot_general(inputs, pre_gate_grad, (((0,), (0,)), ((), ())), preferred_element_type=jnp.float32)
    up_weight_grad = lax.dot_general(inputs, pre_up_grad, (((0,), (0,)), ((), ())), preferred_element_type=jnp.float32)
    return input_grad.astype(jnp.bfloat16), gate_weight_grad, up_weight_grad


def regroup(array):
    rest = array.shape[1:]
    shaped = array.reshape((N_EXPERT, N_REPLICA, TOK_DEV) + rest)
    return jnp.swapaxes(shaped, 0, 1).reshape((N_REPLICA, N_EXPERT * TOK_DEV) + rest)


def ungroup(array):
    rest = array.shape[2:]
    shaped = array.reshape((N_REPLICA, N_EXPERT, TOK_DEV) + rest)
    return jnp.swapaxes(shaped, 0, 1).reshape((N_EXPERT * N_REPLICA * TOK_DEV,) + rest)


def reference(tokens, cotangent, gates, routes, w_gate, w_up, w_down):
    capacity = N_EXPERT * MOST
    route_total = N_EXPERT * TOK_DEV * TOP

    def one_group(carry, packed):
        inputs_group, upstream_group, gates_group, routes_group = packed
        flat_ids = routes_group.reshape(-1)
        flat_gates = gates_group.reshape(-1)

        def one_expert(inner, expert):
            rows_acc, gates_acc = inner
            chosen = flat_ids == expert
            order = (jnp.cumsum(chosen.astype(jnp.int32)) - 1).astype(jnp.int32)
            destination = jnp.where(chosen, order, capacity).astype(jnp.int32)
            source_of = jnp.zeros((capacity + 1,), jnp.int32).at[destination].set(jnp.arange(route_total, dtype=jnp.int32))[:capacity]
            present = jnp.zeros((capacity + 1,), jnp.bfloat16).at[destination].set(jnp.ones((route_total,), jnp.bfloat16))[:capacity]
            token_of = (source_of // TOP).astype(jnp.int32)
            inputs = inputs_group[token_of] * present[:, None]
            upstream = upstream_group[token_of] * present[:, None]
            weights_row = flat_gates[source_of] * present
            gate_matrix = w_gate[expert]
            up_matrix = w_up[expert]
            down_matrix = w_down[expert]
            gate_pre, up_pre, sigmoid_gate, activated, scaled, gate_grad, down_grad = first_phase(
                inputs, upstream, weights_row, gate_matrix, up_matrix, down_matrix)
            input_grad, gate_weight_grad, up_weight_grad = second_phase(
                inputs, gate_pre, up_pre, sigmoid_gate, activated, scaled, gate_matrix, up_matrix, down_matrix)
            mask = present.astype(jnp.float32)
            rows_acc = rows_acc.at[token_of].add(input_grad.astype(jnp.float32) * mask[:, None])
            gates_acc = gates_acc.at[source_of].add(gate_grad.astype(jnp.float32) * mask)
            return (rows_acc, gates_acc), (gate_weight_grad.astype(jnp.bfloat16), up_weight_grad.astype(jnp.bfloat16), down_grad.astype(jnp.bfloat16))

        start = (jnp.zeros((N_EXPERT * TOK_DEV, D), jnp.float32), jnp.zeros((route_total,), jnp.float32))
        (rows_acc, gates_acc), partials = lax.scan(one_expert, start, jnp.arange(EXPERTS, dtype=jnp.int32))
        gate_sum, up_sum, down_sum = carry
        carry = (gate_sum + partials[0].astype(jnp.float32), up_sum + partials[1].astype(jnp.float32), down_sum + partials[2].astype(jnp.float32))
        return carry, (rows_acc.astype(jnp.bfloat16), gates_acc.astype(jnp.bfloat16).reshape(N_EXPERT * TOK_DEV, TOP))

    start = (jnp.zeros((EXPERTS, D, FF), jnp.float32), jnp.zeros((EXPERTS, D, FF), jnp.float32), jnp.zeros((EXPERTS, FF, D), jnp.float32))
    sums, (rows_all, gates_all) = lax.scan(one_group, start, (regroup(tokens), regroup(cotangent), regroup(gates), regroup(routes)))
    return (ungroup(rows_all), ungroup(gates_all), sums[0].astype(jnp.bfloat16), sums[1].astype(jnp.bfloat16), sums[2].astype(jnp.bfloat16))
```

```python
import jax
import jax.numpy as jnp
from jax import lax
from jax.sharding import PartitionSpec as P

MOST = 48
SIDE = 4
DIMS = 4
GRAY = (0, 1, 3, 2)


def flip(axis, bit):
    other = (1, 0, 3, 2) if bit == 0 else (3, 2, 1, 0)
    pairs = []
    for y in range(SIDE):
        for x in range(SIDE):
            ny, nx = (y, other[x]) if axis == "x" else (other[y], x)
            pairs.append((y * SIDE + x, ny * SIDE + nx))
    return pairs


PERMS = (flip("x", 0), flip("y", 0), flip("x", 1), flip("y", 1))


def cube_of(device):
    gx, gy = GRAY[device % SIDE], GRAY[device // SIDE]
    return (gx & 1) | ((gy & 1) << 1) | ((gx >> 1) << 2) | ((gy >> 1) << 3)


CUBE = [cube_of(d) for d in range(16)]
DEVICE = [CUBE.index(c) for c in range(16)]


def slot_at(position, quarter):
    return sum(((position >> s) & 1) << ((quarter + s) % DIMS) for s in range(DIMS))


def swap(x, dim):
    return lax.ppermute(x, "expert", PERMS[dim])


def dot(a, b, contract_a, contract_b):
    return lax.dot_general(
        a, b, (((contract_a,), (contract_b,)), ((), ())), preferred_element_type=jnp.float32
    )


def one_hots(routes_rel, expert_ids):
    hit = jnp.any(routes_rel[:, None] == expert_ids[None, :, None, None], axis=-1)
    tok = routes_rel.shape[1]
    before = jnp.arange(tok)[:, None] < jnp.arange(tok)[None, :]
    rank = jnp.einsum(
        "net,tu->neu",
        hit.astype(jnp.bfloat16),
        before.astype(jnp.bfloat16),
        preferred_element_type=jnp.float32,
    )
    at = jnp.where(hit, rank, -1.0)
    rows = jnp.arange(MOST, dtype=jnp.float32)
    return (at[:, :, None, :] == rows[None, None, :, None]).astype(jnp.bfloat16)


def gather_rows(x, own_hots, partner_hots):
    width = x.shape[1] // DIMS
    near = [x[None, :, width * q : width * (q + 1)] for q in range(DIMS)]
    for s in range(DIMS - 1):
        got = [swap(near[q], (q + s) % DIMS) for q in range(DIMS)]
        near = [jnp.concatenate([a, b], axis=0) for a, b in zip(near, got)]
    parts = []
    for q in range(DIMS):
        send = jnp.einsum(
            "pert,ptd->eprd", partner_hots[q], near[q], preferred_element_type=jnp.float32
        ).astype(jnp.bfloat16)
        far = swap(send, (q + 3) % DIMS)
        hots = jnp.stack([own_hots[slot_at(p, q)] for p in range(8)])
        mine = jnp.einsum("pert,ptd->eprd", hots, near[q], preferred_element_type=jnp.float32)
        rows = jnp.concatenate([mine.astype(jnp.bfloat16), far], axis=1)
        where = [slot_at(p, q) for p in range(16)]
        parts.append(jnp.stack([rows[:, where.index(j)] for j in range(16)], axis=1))
    return jnp.concatenate(parts, axis=-1)


def per_device(tokens, cotangent, gates, routes, w_gate, w_up, w_down):
    tok, fanout = routes.shape
    width = tokens.shape[1]
    quarter = width // DIMS
    me = lax.axis_index("expert")
    cube = jnp.asarray(CUBE, jnp.int32)[me]
    device_of = jnp.asarray(DEVICE, jnp.int32)

    small = jnp.concatenate([gates, routes.astype(jnp.bfloat16)], axis=1)
    small = lax.all_gather(small, "expert", axis=0, tiled=False)
    small = small[device_of[cube ^ jnp.arange(16)]]
    gates_rel = small[:, :, :fanout]
    routes_rel = small[:, :, fanout:].astype(jnp.int32)

    local = jnp.arange(2, dtype=jnp.int32)
    mine = 2 * me + local
    own_hots = one_hots(routes_rel, mine)
    partner_hots = []
    for q in range(DIMS):
        partner = 2 * device_of[cube ^ (1 << ((q + 3) % DIMS))] + local
        near = jnp.stack([routes_rel[slot_at(p, q)] for p in range(8)])
        partner_hots.append(one_hots(near, partner))

    chosen = routes_rel[:, None] == mine[None, :, None, None]
    gate_tok = jnp.sum(jnp.where(chosen, gates_rel[:, None].astype(jnp.float32), 0.0), axis=-1)
    gate_rows = jnp.einsum(
        "jert,jet->ejr",
        own_hots,
        gate_tok.astype(jnp.bfloat16),
        preferred_element_type=jnp.float32,
    ).reshape(2, -1)

    rows = gather_rows(tokens, own_hots, partner_hots).reshape(2, -1, width)
    upstream = gather_rows(cotangent, own_hots, partner_hots).reshape(2, -1, width)

    input_rows, gate_grads, weight_grads = [], [], []
    for e in range(2):
        gate_pre = dot(rows[e], w_gate[e], 1, 0)
        up_pre = dot(rows[e], w_up[e], 1, 0)
        sig = jax.nn.sigmoid(gate_pre)
        act = gate_pre * sig
        hidden = (act * up_pre).astype(jnp.bfloat16)
        back = dot(upstream[e], w_down[e], 1, 1)
        gate_grads.append(jnp.sum(hidden.astype(jnp.float32) * back, axis=1))
        weight = gate_rows[e][:, None]
        grad_hidden = back * weight
        d_gate = (grad_hidden * up_pre * sig * (1.0 + gate_pre * (1.0 - sig))).astype(jnp.bfloat16)
        d_up = (grad_hidden * act).astype(jnp.bfloat16)
        scaled = (hidden.astype(jnp.float32) * weight).astype(jnp.bfloat16)
        weight_grads += [
            dot(rows[e], d_gate, 0, 0),
            dot(rows[e], d_up, 0, 0),
            dot(upstream[e], scaled, 0, 0),
        ]
        input_rows.append((dot(d_gate, w_gate[e], 1, 1) + dot(d_up, w_up[e], 1, 1)))

    totals = lax.psum_scatter(
        jnp.stack(weight_grads).astype(jnp.bfloat16), "replica", scatter_dimension=1, tiled=True
    )

    gate_grads = jnp.stack(gate_grads).reshape(2, 16, MOST)
    gate_back = jnp.einsum(
        "jert,ejr->jet",
        own_hots,
        gate_grads.astype(jnp.bfloat16),
        preferred_element_type=jnp.float32,
    ).astype(jnp.bfloat16)
    gate_back = gate_back[cube ^ jnp.asarray(CUBE, jnp.int32)]
    gate_back = lax.all_to_all(gate_back, "expert", split_axis=0, concat_axis=0, tiled=True)
    by_expert = gate_back.reshape(32, tok)
    picked = routes[:, None, :] == jnp.arange(32, dtype=jnp.int32)[None, :, None]
    grad_gates = jnp.sum(
        jnp.where(picked, by_expert.T[:, :, None].astype(jnp.float32), 0.0), axis=1
    ).astype(jnp.bfloat16)

    input_rows = jnp.stack(input_rows).astype(jnp.bfloat16).reshape(2, 16, MOST, width)
    parts = []
    for q in range(DIMS):
        part = input_rows[..., quarter * q : quarter * (q + 1)]
        slots = [slot_at(p, q) for p in range(16)]
        far = jnp.stack([part[:, slots[p + 8]] for p in range(8)], axis=1)
        near = jnp.stack([part[:, slots[p]] for p in range(8)], axis=1)
        got = swap(far, (q + 3) % DIMS)
        hots = jnp.stack([own_hots[slots[p]] for p in range(8)])
        total = jnp.einsum("pert,eprd->ptd", hots, near, preferred_element_type=jnp.float32)
        total = total + jnp.einsum(
            "pert,eprd->ptd", partner_hots[q], got, preferred_element_type=jnp.float32
        )
        total = total.astype(jnp.bfloat16)
        for s in (2, 1, 0):
            half = 1 << s
            got = swap(total[half:], (q + s) % DIMS)
            total = (total[:half].astype(jnp.float32) + got.astype(jnp.float32)).astype(
                jnp.bfloat16
            )
        parts.append(total[0])
    grad_input = jnp.concatenate(parts, axis=1)
    return (
        grad_input,
        grad_gates,
        totals[0::3],
        totals[1::3],
        jnp.swapaxes(totals[2::3], 1, 2),
    )


def solution(mesh):
    tok = P(("expert", "replica"), None)
    return jax.shard_map(
        per_device,
        mesh=mesh,
        in_specs=(tok, tok, tok, tok) + (P("expert", None, None),) * 3,
        out_specs=(
            tok,
            tok,
            P("expert", "replica", None),
            P("expert", "replica", None),
            P("expert", None, "replica"),
        ),
        check_vma=False,
    )
```

```python
import jax
import jax.numpy as jnp
from jax import lax
from jax.experimental import pallas as pl
from jax.experimental.pallas import tpu as pltpu
from jax.sharding import PartitionSpec as P

MOST = 48
SIDE = 4
DIMS = 4
GRAY = (0, 1, 3, 2)


def flip(axis, bit):
    other = (1, 0, 3, 2) if bit == 0 else (3, 2, 1, 0)
    pairs = []
    for y in range(SIDE):
        for x in range(SIDE):
            ny, nx = (y, other[x]) if axis == "x" else (other[y], x)
            pairs.append((y * SIDE + x, ny * SIDE + nx))
    return pairs


PERMS = (flip("x", 0), flip("y", 0), flip("x", 1), flip("y", 1))


def cube_of(device):
    gx, gy = GRAY[device % SIDE], GRAY[device // SIDE]
    return (gx & 1) | ((gy & 1) << 1) | ((gx >> 1) << 2) | ((gy >> 1) << 3)


CUBE = [cube_of(d) for d in range(16)]
DEVICE = [CUBE.index(c) for c in range(16)]


def slot_at(position, quarter):
    return sum(((position >> s) & 1) << ((quarter + s) % DIMS) for s in range(DIMS))


def swap(x, dim):
    return lax.ppermute(x, "expert", PERMS[dim])


def one_hots(routes_rel, expert_ids):
    hit = jnp.any(routes_rel[:, None] == expert_ids[None, :, None, None], axis=2)
    tok = routes_rel.shape[2]
    before = jnp.arange(tok)[:, None] < jnp.arange(tok)[None, :]
    rank = jnp.einsum(
        "net,tu->neu",
        hit.astype(jnp.bfloat16),
        before.astype(jnp.bfloat16),
        preferred_element_type=jnp.float32,
    )
    at = jnp.where(hit, rank, -1.0)
    rows = jnp.arange(MOST, dtype=jnp.float32)
    return (at[:, :, None, :] == rows[None, None, :, None]).astype(jnp.bfloat16)


EXTRA = 16


def gather_rows(tokens, cotangent, small):
    width = tokens.shape[1] // DIMS
    small = small.reshape(-1, width)
    small = jnp.concatenate([small, jnp.zeros((EXTRA - small.shape[0], width), small.dtype)])
    near = []
    for q in range(DIMS):
        cols = slice(width * q, width * (q + 1))
        near.append(jnp.concatenate([tokens[:, cols], cotangent[:, cols], small])[None])
    for s in range(DIMS - 1):
        got = [swap(near[q], (q + s) % DIMS) for q in range(DIMS)]
        if s == DIMS - 2:
            return list(zip(near, got))
        near = [jnp.concatenate([a, b], axis=0) for a, b in zip(near, got)]


def dispatch_kernel(q, device_ref, low, high, send_a, send_b, own_a, own_b, hots):
    count, rows, width = low.shape
    tok = (rows - EXTRA) // 2
    per_row = width // tok
    here = device_ref[0]
    partner = device_ref[1 << ((q + 3) % DIMS)]
    lower = lax.broadcasted_iota(jnp.int32, (tok, tok), 0)
    before = (lower < lax.broadcasted_iota(jnp.int32, (tok, tok), 1)).astype(jnp.bfloat16)
    index = lax.broadcasted_iota(jnp.int32, (MOST, tok), 0).astype(jnp.float32)

    def half(near):
        hits = []
        for p in range(count):
            small = near[p, 2 * tok :, :].astype(jnp.float32)
            routes = jnp.concatenate(
                [
                    small[i // per_row : i // per_row + 1, i % per_row * tok : (i % per_row + 1) * tok]
                    for i in range(8, 16)
                ],
                axis=0,
            )
            for target in (here, partner):
                for local in range(2):
                    expert = (2 * target + local).astype(jnp.float32)
                    same = (routes == expert).astype(jnp.float32)
                    hits.append(jnp.max(same, axis=0, keepdims=True))
        hit = jnp.concatenate(hits, axis=0)
        rank = jnp.dot(hit.astype(jnp.bfloat16), before, preferred_element_type=jnp.float32)
        at = jnp.where(hit > 0.0, rank, -1.0)
        for p in range(count):
            hot = jnp.concatenate(
                [(index == at[4 * p + i : 4 * p + i + 1]).astype(jnp.bfloat16) for i in range(4)],
                axis=0,
            )
            hots[p] = hot
            for which, (own, send) in enumerate(((own_a, send_a), (own_b, send_b))):
                out = jnp.dot(
                    hot, near[p, which * tok : (which + 1) * tok], preferred_element_type=jnp.float32
                )
                out = out.astype(jnp.bfloat16)
                for local in range(2):
                    own[p, local] = out[local * MOST : (local + 1) * MOST]
                    send[p, local] = out[(2 + local) * MOST : (3 + local) * MOST]

    @pl.when(pl.program_id(0) == 0)
    def _():
        half(low)

    @pl.when(pl.program_id(0) == 1)
    def _():
        half(high)


def dispatch(q, devices, low, high):
    block, length, width = low.shape
    tok = (length - EXTRA) // 2
    count = 2 * block
    rows = (count, 2, MOST, width)
    row_block = pl.BlockSpec((block,) + rows[1:], lambda i, d: (i, 0, 0, 0))
    whole = pl.BlockSpec(low.shape, lambda i, d: (0, 0, 0))

    def kernel(*refs):
        dispatch_kernel(q, *refs)

    return pl.pallas_call(
        kernel,
        grid_spec=pltpu.PrefetchScalarGridSpec(
            num_scalar_prefetch=1,
            grid=(2,),
            in_specs=[whole, whole],
            out_specs=[row_block] * 4
            + [pl.BlockSpec((block, 4 * MOST, tok), lambda i, d: (i, 0, 0))],
        ),
        out_shape=[jax.ShapeDtypeStruct(rows, jnp.bfloat16)] * 4
        + [jax.ShapeDtypeStruct((count, 4 * MOST, tok), jnp.bfloat16)],
        compiler_params=params(58),
        cost_estimate=pl.CostEstimate(
            flops=2 * count * 2 * 4 * MOST * tok * width,
            bytes_accessed=6 << 20,
            transcendentals=0,
        ),
        name="dispatch",
    )(devices, low, high)


def combine_kernel(hots, own, got, keep, send):
    count = own.shape[0]

    def fill(out):
        for p in range(count):
            rows = jnp.concatenate([own[p, 0], own[p, 1], got[p, 0], got[p, 1]], axis=0)
            out[p] = lax.dot_general(
                hots[p], rows, (((0,), (0,)), ((), ())), preferred_element_type=jnp.float32
            ).astype(jnp.bfloat16)

    @pl.when(pl.program_id(0) == 0)
    def _():
        fill(send)

    @pl.when(pl.program_id(0) == 1)
    def _():
        fill(keep)


def combine(hots, own, got):
    count, _, _, width = own.shape
    tok = hots.shape[2]
    block = count // 2
    row_block = pl.BlockSpec((block,) + own.shape[1:], lambda i: (1 - i, 0, 0, 0))
    out = pl.BlockSpec((block, tok, width), lambda i: (0, 0, 0))
    return pl.pallas_call(
        combine_kernel,
        grid=(2,),
        in_specs=[
            pl.BlockSpec((block,) + hots.shape[1:], lambda i: (1 - i, 0, 0)),
            row_block,
            row_block,
        ],
        out_specs=[out, out],
        out_shape=[jax.ShapeDtypeStruct((block, tok, width), jnp.bfloat16)] * 2,
        compiler_params=params(24),
        cost_estimate=pl.CostEstimate(
            flops=2 * count * 4 * MOST * tok * width, bytes_accessed=4 << 20, transcendentals=0
        ),
        name="combine",
    )(hots, own, got)


def by_bits(rows):
    return rows.reshape((2, 2, 2) + rows.shape[1:])


def row_copies(parts, rows, sems, e):
    copies = []
    for q in range(DIMS):
        for bit in range(2):
            part = parts[q + DIMS * bit]
            width = part.shape[-1]
            cols = pl.ds(q * width, width)
            if q == 0:
                pairs = [(part.at[:, :, :, e], rows.at[e, bit, :, :, :, :, cols])]
            elif q == 1:
                pairs = [(part.at[:, :, :, e], rows.at[e, :, :, :, bit, :, cols])]
            elif q == 2:
                pairs = [
                    (part.at[low, :, :, e], rows.at[e, :, :, bit, low, :, cols])
                    for low in range(2)
                ]
            else:
                pairs = [
                    (part.at[mid, low, :, e], rows.at[e, :, bit, mid, low, :, cols])
                    for mid in range(2)
                    for low in range(2)
                ]
            for source, target in pairs:
                copies.append(pltpu.make_async_copy(source, target, sems.at[e, len(copies)]))
    return copies


COPIES = 16


def load_rows(parts, rows, sems):
    e = pl.program_id(0)

    @pl.when(e == 0)
    def _():
        for which in range(2):
            for copy in row_copies(parts, rows, sems, which):
                copy.start()

    for which in range(2):

        @pl.when(e == which)
        def _():
            for copy in row_copies(parts, rows, sems, which):
                copy.wait()

    here = rows[e]
    return here.reshape(-1, here.shape[-1])


def nt(a, b):
    return lax.dot_general(a, b, (((1,), (1,)), ((), ())), preferred_element_type=jnp.float32)


def nn(a, b):
    return jnp.dot(a, b, preferred_element_type=jnp.float32)


def tn(a, b):
    return lax.dot_general(a, b, (((0,), (0,)), ((), ())), preferred_element_type=jnp.float32)


def forward_kernel(*refs):
    parts, (w_gate, w_up), outs = refs[:8], refs[8:10], refs[10:13]
    rows, sems = refs[13:]
    hidden_ref, gate_slope, act_ref = outs
    here = load_rows(parts, rows, sems)
    gate_pre = nn(here, w_gate[0])
    up_pre = nn(here, w_up[0])
    sig = jax.nn.sigmoid(gate_pre)
    act = gate_pre * sig
    hidden_ref[0] = (act * up_pre).astype(jnp.bfloat16)
    slope = up_pre * sig * (1.0 + gate_pre * (1.0 - sig))
    gate_slope[0] = slope.astype(jnp.bfloat16)
    act_ref[0] = act.astype(jnp.bfloat16)


def backward_kernel(*refs):
    tokens, upstream, ins, outs = refs[:8], refs[8:16], refs[16:21], refs[21:25]
    w_down, hidden, gate_slope, act, gate_rows = ins
    grads, d_gate_out, d_up_out, gate_out = outs
    x, c, c_sems, x_sems, in_sems, out_sems = refs[25:31]
    w_v, hidden_v, slope_v, act_v, rows_v = refs[31:36]
    grads_v, d_gate_v, d_up_v, gate_v = refs[36:40]
    n = w_v.shape[0]
    shards, _, block, ff = grads_v.shape

    def inputs(e):
        pairs = ((w_down, w_v), (hidden, hidden_v), (gate_slope, slope_v), (act, act_v))
        pairs = pairs + ((gate_rows, rows_v),)
        return [
            pltpu.make_async_copy(source.at[e], target.at[e], in_sems.at[e, i])
            for i, (source, target) in enumerate(pairs)
        ]

    def outputs(e):
        pairs = [(grads_v.at[:, 3 * e + m], grads.at[:, 3 * e + m]) for m in range(3)]
        pairs += [
            (d_gate_v.at[e], d_gate_out.at[e]),
            (d_up_v.at[e], d_up_out.at[e]),
            (gate_v.at[e], gate_out.at[e]),
        ]
        return [
            pltpu.make_async_copy(source, target, out_sems.at[e, i])
            for i, (source, target) in enumerate(pairs)
        ]

    def begin(e):
        copies = inputs(e)
        copies[0].start()
        for copy in row_copies(upstream, c, c_sems, e):
            copy.start()
        for copy in copies[1:]:
            copy.start()

    begin(0)
    for e in range(n):
        copies = inputs(e)
        done = outputs(e)
        copies[0].wait()
        for copy in row_copies(upstream, c, c_sems, e):
            copy.wait()
        for copy in row_copies(tokens, x, x_sems, e):
            copy.start()
        here = c[e]
        here = here.reshape(-1, here.shape[-1])
        back = nt(here, w_v[e])
        for copy in copies[1:]:
            copy.wait()
        saved = hidden_v[e].astype(jnp.float32)
        lanes = rows_v.shape[2]
        weight = jnp.concatenate([rows_v[e].astype(jnp.float32)] * (ff // lanes), axis=1)
        terms = saved * back
        gate_v[e] = sum(terms[:, i : i + lanes] for i in range(0, ff, lanes))
        back = back * weight
        d_gate = (back * slope_v[e].astype(jnp.float32)).astype(jnp.bfloat16)
        d_up = (back * act_v[e].astype(jnp.float32)).astype(jnp.bfloat16)
        scaled = (saved * weight).astype(jnp.bfloat16)
        d_gate_v[e] = d_gate
        d_up_v[e] = d_up
        for i in (3, 4, 5):
            done[i].start()
        for r in range(shards):
            total = tn(scaled, here[:, r * block : (r + 1) * block]).astype(jnp.bfloat16)
            for half in range(ff // block):
                grads_v[r, 3 * e + 2, :, half * block : (half + 1) * block] = total[
                    half * block : (half + 1) * block
                ]
        for copy in row_copies(tokens, x, x_sems, e):
            copy.wait()
        if e + 1 < n:
            begin(e + 1)
        done[2].start()
        here = x[e]
        here = here.reshape(-1, here.shape[-1])
        for m, slope in ((0, d_gate), (1, d_up)):
            for r in range(shards):
                total = tn(here[:, r * block : (r + 1) * block], slope)
                grads_v[r, 3 * e + m] = total.astype(jnp.bfloat16)
            done[m].start()
    for e in range(n):
        for copy in outputs(e):
            copy.wait()


def input_kernel(*refs):
    d_gate, d_up, w_gate, w_up = refs[:4]
    outs = refs[4:12]
    gate_v, up_v, w_gate_v, w_up_v, out_v, d_sems, w_sems, out_sems = refs[12:]
    n, _, quarter, _ = w_gate_v.shape[1:]

    def weights(q):
        cols = pl.ds(q * quarter, quarter)
        return [
            pltpu.make_async_copy(source.at[:, cols], target.at[q % 2, :, 0], w_sems.at[q, i])
            for i, (source, target) in enumerate(((w_gate, w_gate_v), (w_up, w_up_v)))
        ]

    def results(q):
        return [
            pltpu.make_async_copy(out_v.at[q, i], outs[q + DIMS * i], out_sems.at[q, i])
            for i in range(2)
        ]

    slopes = [
        pltpu.make_async_copy(d_gate, gate_v, d_sems.at[0]),
        pltpu.make_async_copy(d_up, up_v, d_sems.at[1]),
    ]
    for copy in slopes + weights(0) + weights(1):
        copy.start()
    for copy in slopes:
        copy.wait()
    for q in range(DIMS):
        for copy in weights(q):
            copy.wait()
        for e in range(n):
            total = nt(gate_v[e], w_gate_v[q % 2, e, 0]) + nt(up_v[e], w_up_v[q % 2, e, 0])
            total = total.astype(jnp.bfloat16)
            for p in range(16):
                slot = slot_at(p, q)
                out_v[q, 1 - p // 8, p % 8, e] = total[slot * MOST : (slot + 1) * MOST]
        for copy in results(q):
            copy.start()
        if q + 2 < DIMS:
            for copy in weights(q + 2):
                copy.start()
    for q in range(DIMS):
        for copy in results(q):
            copy.wait()


def one(shape):
    zeros = (0,) * (len(shape) - 1)
    return pl.BlockSpec((1,) + tuple(shape[1:]), lambda e: (e,) + zeros)


def params(mib):
    return pltpu.CompilerParams(
        dimension_semantics=("arbitrary",), vmem_limit_bytes=mib * 1024 * 1024
    )


def forward(parts, w_gate, w_up):
    n, width, ff = w_gate.shape
    count = 16 * MOST
    shapes = [
        ((n, count, ff), jnp.bfloat16),
        ((n, count, ff), jnp.bfloat16),
        ((n, count, ff), jnp.bfloat16),
    ]
    return pl.pallas_call(
        forward_kernel,
        grid=(n,),
        in_specs=[pl.BlockSpec(memory_space=pl.ANY)] * 8 + [one(w_gate.shape), one(w_up.shape)],
        out_specs=[one(s) for s, _ in shapes],
        out_shape=[jax.ShapeDtypeStruct(s, t) for s, t in shapes],
        scratch_shapes=[
            pltpu.VMEM((n, 2, 2, 2, 2, MOST, width), jnp.bfloat16),
            pltpu.SemaphoreType.DMA((n, COPIES)),
        ],
        compiler_params=params(48),
        cost_estimate=pl.CostEstimate(
            flops=4 * n * count * width * ff, bytes_accessed=36 << 20, transcendentals=0
        ),
        name="forward",
    )(*parts, w_gate, w_up)


def backward(tokens, upstream, w_down, saved, gate_rows, shards):
    n, ff, width = w_down.shape
    count = gate_rows.shape[1]
    hidden, gate_slope, act = saved
    shapes = [
        ((shards, 3 * n, width // shards, ff), jnp.bfloat16),
        ((n, count, ff), jnp.bfloat16),
        ((n, count, ff), jnp.bfloat16),
        ((n, count, gate_rows.shape[2]), jnp.float32),
    ]
    ins = (w_down, hidden, gate_slope, act, gate_rows)
    rows = pltpu.VMEM((n, 2, 2, 2, 2, MOST, width), jnp.bfloat16)
    return pl.pallas_call(
        backward_kernel,
        in_specs=[pl.BlockSpec(memory_space=pl.ANY)] * 21,
        out_specs=[pl.BlockSpec(memory_space=pl.ANY)] * 4,
        out_shape=[jax.ShapeDtypeStruct(s, t) for s, t in shapes],
        scratch_shapes=[
            rows,
            rows,
            pltpu.SemaphoreType.DMA((n, COPIES)),
            pltpu.SemaphoreType.DMA((n, COPIES)),
            pltpu.SemaphoreType.DMA((n, 5)),
            pltpu.SemaphoreType.DMA((n, 6)),
        ]
        + [pltpu.VMEM(x.shape, x.dtype) for x in ins]
        + [pltpu.VMEM(s, t) for s, t in shapes],
        compiler_params=pltpu.CompilerParams(vmem_limit_bytes=58 << 20),
        cost_estimate=pl.CostEstimate(
            flops=8 * n * count * width * ff, bytes_accessed=50 << 20, transcendentals=0
        ),
        name="backward",
    )(*tokens, *upstream, *ins)


def input_rows(d_gate, d_up, w_gate, w_up):
    n, width, ff = w_gate.shape
    count = d_gate.shape[1]
    quarter = width // DIMS
    shape = (8, n, MOST, quarter)
    weight = pltpu.VMEM((2, n, 1, quarter, ff), jnp.bfloat16)
    out = pl.pallas_call(
        input_kernel,
        in_specs=[pl.BlockSpec(memory_space=pl.ANY)] * 4,
        out_specs=[pl.BlockSpec(memory_space=pl.ANY)] * 8,
        out_shape=[jax.ShapeDtypeStruct(shape, jnp.bfloat16)] * 8,
        scratch_shapes=[
            pltpu.VMEM(d_gate.shape, jnp.bfloat16),
            pltpu.VMEM(d_up.shape, jnp.bfloat16),
            weight,
            weight,
            pltpu.VMEM((DIMS, 2) + shape, jnp.bfloat16),
            pltpu.SemaphoreType.DMA((2,)),
            pltpu.SemaphoreType.DMA((DIMS, 2)),
            pltpu.SemaphoreType.DMA((DIMS, 2)),
        ],
        compiler_params=pltpu.CompilerParams(vmem_limit_bytes=56 << 20),
        cost_estimate=pl.CostEstimate(
            flops=4 * n * count * width * ff, bytes_accessed=24 << 20, transcendentals=0
        ),
        name="input_rows",
    )(d_gate, d_up, w_gate, w_up)
    return out[:DIMS], out[DIMS:]


def per_device(tokens, cotangent, gates, routes, w_gate, w_up, w_down):
    tok, fanout = routes.shape
    me = lax.axis_index("expert")
    cube = jnp.asarray(CUBE, jnp.int32)[me]
    device_of = jnp.asarray(DEVICE, jnp.int32)

    info = jnp.concatenate([gates, routes.astype(jnp.bfloat16)], axis=1).T
    small = jnp.concatenate([info, jnp.zeros((240, tok), jnp.bfloat16)], axis=0)
    small = lax.all_gather(small, "expert", axis=0, tiled=False)[:, :16]
    near = gather_rows(tokens, cotangent, info)
    devices = device_of[cube ^ jnp.arange(16)]
    small = small[devices]
    gates_rel = small[:, :fanout]
    routes_rel = small[:, fanout:].astype(jnp.int32)

    local = jnp.arange(2, dtype=jnp.int32)
    mine = 2 * me + local
    own_hots = one_hots(routes_rel, mine)
    chosen = routes_rel[:, None] == mine[None, :, None, None]
    gate_tok = jnp.sum(jnp.where(chosen, gates_rel[:, None].astype(jnp.float32), 0.0), axis=2)
    gate_rows = jnp.einsum(
        "jert,jet->ejr",
        own_hots,
        gate_tok.astype(jnp.bfloat16),
        preferred_element_type=jnp.float32,
    ).reshape(2, -1, 1)
    gate_rows = jnp.broadcast_to(gate_rows.astype(jnp.bfloat16), gate_rows.shape[:2] + (tok,))

    picked = [dispatch(q, devices, *near[q]) for q in range(DIMS)]
    firsts = [swap(picked[q][0], (q + 3) % DIMS) for q in range(DIMS)]
    seconds = []
    for q in range(DIMS):
        send, firsts[q] = lax.optimization_barrier((picked[q][1], firsts[q]))
        seconds.append(swap(send, (q + 3) % DIMS))
    token_parts = [by_bits(x) for x in [d[2] for d in picked] + firsts]
    upstream_parts = [by_bits(x) for x in [d[3] for d in picked] + seconds]
    hots = [d[4] for d in picked]
    saved = forward(token_parts, w_gate, w_up)
    shards = lax.axis_size("replica")
    grads, d_gate, d_up, gate_grads = backward(
        token_parts, upstream_parts, w_down, saved, gate_rows, shards
    )
    totals = lax.psum_scatter(grads, "replica", scatter_dimension=0, tiled=False)

    fars, rows = input_rows(d_gate, d_up, w_gate, w_up)
    fars, gate_grads = lax.optimization_barrier((fars, gate_grads))

    gate_back = jnp.einsum(
        "jert,ejr->jet",
        own_hots,
        jnp.sum(gate_grads, axis=2).reshape(2, 16, MOST).astype(jnp.bfloat16),
        preferred_element_type=jnp.float32,
    ).astype(jnp.bfloat16)
    gate_back = gate_back[cube ^ jnp.asarray(CUBE, jnp.int32)]
    gate_back = lax.all_to_all(gate_back, "expert", split_axis=0, concat_axis=0, tiled=True)
    by_expert = gate_back.reshape(32, tok)
    chosen = routes[:, None, :] == jnp.arange(32, dtype=jnp.int32)[None, :, None]
    grad_gates = jnp.sum(
        jnp.where(chosen, by_expert.T[:, :, None].astype(jnp.float32), 0.0), axis=1
    ).astype(jnp.bfloat16)

    parts = []
    for q in range(DIMS):
        got = swap(fars[q], (q + 3) % DIMS)
        keep, send = combine(hots[q], rows[q], got)
        for s in (2, 1, 0):
            got = swap(send, (q + s) % DIMS)
            half = keep.shape[0] // 2
            if s:
                send = (keep[half:].astype(jnp.float32) + got[half:].astype(jnp.float32)).astype(
                    jnp.bfloat16
                )
                keep, got = keep[:half], got[:half]
            keep = (keep.astype(jnp.float32) + got.astype(jnp.float32)).astype(jnp.bfloat16)
        parts.append(keep[0])
    grad_input = jnp.concatenate(parts, axis=1)
    down = totals[2::3]
    block = down.shape[1]
    down = jnp.concatenate(
        [down[:, :, block * half : block * (half + 1)] for half in range(down.shape[2] // block)],
        axis=1,
    )
    return grad_input, grad_gates, totals[0::3], totals[1::3], down


def solution(mesh):
    tok = P(("expert", "replica"), None)
    return jax.shard_map(
        per_device,
        mesh=mesh,
        in_specs=(tok, tok, tok, tok) + (P("expert", None, None),) * 3,
        out_specs=(
            tok,
            tok,
            P("expert", "replica", None),
            P("expert", "replica", None),
            P("expert", None, "replica"),
        ),
        check_vma=False,
    )
```

```python
import jax
import jax.numpy as jnp
from jax import lax
from jax.experimental import pallas as pl
from jax.experimental.pallas import tpu as pltpu
from jax.sharding import PartitionSpec as P

MOST = 48
SIDE = 4
DIMS = 4
GRAY = (0, 1, 3, 2)


def flip(axis, bit):
    other = (1, 0, 3, 2) if bit == 0 else (3, 2, 1, 0)
    pairs = []
    for y in range(SIDE):
        for x in range(SIDE):
            ny, nx = (y, other[x]) if axis == "x" else (other[y], x)
            pairs.append((y * SIDE + x, ny * SIDE + nx))
    return pairs


PERMS = (flip("x", 0), flip("y", 0), flip("x", 1), flip("y", 1))


def cube_of(device):
    gx, gy = GRAY[device % SIDE], GRAY[device // SIDE]
    return (gx & 1) | ((gy & 1) << 1) | ((gx >> 1) << 2) | ((gy >> 1) << 3)


CUBE = [cube_of(d) for d in range(16)]
DEVICE = [CUBE.index(c) for c in range(16)]


def slot_at(position, quarter):
    return sum(((position >> s) & 1) << ((quarter + s) % DIMS) for s in range(DIMS))


def swap(x, dim):
    return lax.ppermute(x, "expert", PERMS[dim])


def one_hots(routes_rel, expert_ids):
    hit = jnp.any(routes_rel[:, None] == expert_ids[None, :, None, None], axis=2)
    tok = routes_rel.shape[2]
    before = jnp.arange(tok)[:, None] < jnp.arange(tok)[None, :]
    rank = jnp.einsum(
        "net,tu->neu",
        hit.astype(jnp.bfloat16),
        before.astype(jnp.bfloat16),
        preferred_element_type=jnp.float32,
    )
    at = jnp.where(hit, rank, -1.0)
    rows = jnp.arange(MOST, dtype=jnp.float32)
    return (at[:, :, None, :] == rows[None, None, :, None]).astype(jnp.bfloat16)


EXTRA = 16


def gather_rows(tokens, cotangent, small):
    width = tokens.shape[1] // DIMS
    small = small.reshape(-1, width)
    small = jnp.concatenate([small, jnp.zeros((EXTRA - small.shape[0], width), small.dtype)])
    near = []
    for q in range(DIMS):
        cols = slice(width * q, width * (q + 1))
        near.append(jnp.concatenate([tokens[:, cols], cotangent[:, cols], small])[None])
    for s in range(DIMS - 1):
        got = [swap(near[q], (q + s) % DIMS) for q in range(DIMS)]
        if s == DIMS - 2:
            return list(zip(near, got))
        near = [jnp.concatenate([a, b], axis=0) for a, b in zip(near, got)]


def dispatch_kernel(q, device_ref, low, high, send_a, send_b, own_a, own_b, hots):
    count, rows, width = low.shape
    tok = (rows - EXTRA) // 2
    per_row = width // tok
    here = device_ref[0]
    partner = device_ref[1 << ((q + 3) % DIMS)]
    lower = lax.broadcasted_iota(jnp.int32, (tok, tok), 0)
    before = (lower < lax.broadcasted_iota(jnp.int32, (tok, tok), 1)).astype(jnp.bfloat16)
    index = lax.broadcasted_iota(jnp.int32, (MOST, tok), 0).astype(jnp.float32)

    def half(near):
        hits = []
        for p in range(count):
            small = near[p, 2 * tok :, :].astype(jnp.float32)
            routes = jnp.concatenate(
                [
                    small[i // per_row : i // per_row + 1, i % per_row * tok : (i % per_row + 1) * tok]
                    for i in range(8, 16)
                ],
                axis=0,
            )
            for target in (here, partner):
                for local in range(2):
                    expert = (2 * target + local).astype(jnp.float32)
                    same = (routes == expert).astype(jnp.float32)
                    hits.append(jnp.max(same, axis=0, keepdims=True))
        hit = jnp.concatenate(hits, axis=0)
        rank = jnp.dot(hit.astype(jnp.bfloat16), before, preferred_element_type=jnp.float32)
        at = jnp.where(hit > 0.0, rank, -1.0)
        for p in range(count):
            hot = jnp.concatenate(
                [(index == at[4 * p + i : 4 * p + i + 1]).astype(jnp.bfloat16) for i in range(4)],
                axis=0,
            )
            hots[p] = hot
            none = jnp.zeros_like(hot)
            both = jnp.concatenate(
                [
                    jnp.concatenate([hot, none], axis=1),
                    jnp.concatenate([none, hot], axis=1),
                ],
                axis=0,
            )
            out = jnp.dot(both, near[p, : 2 * tok], preferred_element_type=jnp.float32)
            out = out.astype(jnp.bfloat16)
            for i, rows_out in enumerate((own_a, send_a, own_b, send_b)):
                for local in range(2):
                    at_row = (2 * i + local) * MOST
                    rows_out[p, local] = out[at_row : at_row + MOST]

    @pl.when(pl.program_id(0) == 0)
    def _():
        half(low)

    @pl.when(pl.program_id(0) == 1)
    def _():
        half(high)


def dispatch(q, devices, low, high):
    block, length, width = low.shape
    tok = (length - EXTRA) // 2
    count = 2 * block
    rows = (count, 2, MOST, width)
    row_block = pl.BlockSpec((block,) + rows[1:], lambda i, d: (i, 0, 0, 0))
    whole = pl.BlockSpec(low.shape, lambda i, d: (0, 0, 0))

    def kernel(*refs):
        dispatch_kernel(q, *refs)

    return pl.pallas_call(
        kernel,
        grid_spec=pltpu.PrefetchScalarGridSpec(
            num_scalar_prefetch=1,
            grid=(2,),
            in_specs=[whole, whole],
            out_specs=[row_block] * 4
            + [pl.BlockSpec((block, 4 * MOST, tok), lambda i, d: (i, 0, 0))],
        ),
        out_shape=[jax.ShapeDtypeStruct(rows, jnp.bfloat16)] * 4
        + [jax.ShapeDtypeStruct((count, 4 * MOST, tok), jnp.bfloat16)],
        compiler_params=params(58),
        cost_estimate=pl.CostEstimate(
            flops=2 * count * 2 * 4 * MOST * tok * width,
            bytes_accessed=6 << 20,
            transcendentals=0,
        ),
        name="dispatch",
    )(devices, low, high)


def combine_kernel(hots, own, got, keep, send):
    count = own.shape[0]

    def fill(out):
        for p in range(count):
            rows = jnp.concatenate([own[p, 0], own[p, 1], got[p, 0], got[p, 1]], axis=0)
            out[p] = lax.dot_general(
                hots[p], rows, (((0,), (0,)), ((), ())), preferred_element_type=jnp.float32
            ).astype(jnp.bfloat16)

    @pl.when(pl.program_id(0) == 0)
    def _():
        fill(send)

    @pl.when(pl.program_id(0) == 1)
    def _():
        fill(keep)


def combine(hots, own, got):
    count, _, _, width = own.shape
    tok = hots.shape[2]
    block = count // 2
    row_block = pl.BlockSpec((block,) + own.shape[1:], lambda i: (1 - i, 0, 0, 0))
    out = pl.BlockSpec((block, tok, width), lambda i: (0, 0, 0))
    return pl.pallas_call(
        combine_kernel,
        grid=(2,),
        in_specs=[
            pl.BlockSpec((block,) + hots.shape[1:], lambda i: (1 - i, 0, 0)),
            row_block,
            row_block,
        ],
        out_specs=[out, out],
        out_shape=[jax.ShapeDtypeStruct((block, tok, width), jnp.bfloat16)] * 2,
        compiler_params=params(24),
        cost_estimate=pl.CostEstimate(
            flops=2 * count * 4 * MOST * tok * width, bytes_accessed=4 << 20, transcendentals=0
        ),
        name="combine",
    )(hots, own, got)


def by_bits(rows):
    return rows.reshape((2, 2, 2) + rows.shape[1:])


def row_copies(parts, rows, sems, e):
    copies = []
    for q in range(DIMS):
        for bit in range(2):
            part = parts[q + DIMS * bit]
            width = part.shape[-1]
            cols = pl.ds(q * width, width)
            if q == 0:
                pairs = [(part.at[:, :, :, e], rows.at[e, bit, :, :, :, :, cols])]
            elif q == 1:
                pairs = [(part.at[:, :, :, e], rows.at[e, :, :, :, bit, :, cols])]
            elif q == 2:
                pairs = [
                    (part.at[low, :, :, e], rows.at[e, :, :, bit, low, :, cols])
                    for low in range(2)
                ]
            else:
                pairs = [
                    (part.at[mid, low, :, e], rows.at[e, :, bit, mid, low, :, cols])
                    for mid in range(2)
                    for low in range(2)
                ]
            for source, target in pairs:
                copies.append(pltpu.make_async_copy(source, target, sems.at[e, len(copies)]))
    return copies


COPIES = 16


def load_rows(parts, rows, sems):
    e = pl.program_id(0)

    @pl.when(e == 0)
    def _():
        for which in range(2):
            for copy in row_copies(parts, rows, sems, which):
                copy.start()

    for which in range(2):

        @pl.when(e == which)
        def _():
            for copy in row_copies(parts, rows, sems, which):
                copy.wait()

    here = rows[e]
    return here.reshape(-1, here.shape[-1])


def nt(a, b):
    return lax.dot_general(a, b, (((1,), (1,)), ((), ())), preferred_element_type=jnp.float32)


def nn(a, b):
    return jnp.dot(a, b, preferred_element_type=jnp.float32)


def tn(a, b):
    return lax.dot_general(a, b, (((0,), (0,)), ((), ())), preferred_element_type=jnp.float32)


def forward_kernel(*refs):
    parts, (w_gate, w_up), outs = refs[:8], refs[8:10], refs[10:13]
    rows, sems = refs[13:]
    hidden_ref, gate_slope, act_ref = outs
    here = load_rows(parts, rows, sems)
    gate_pre = nn(here, w_gate[0])
    up_pre = nn(here, w_up[0])
    sig = jax.nn.sigmoid(gate_pre)
    act = gate_pre * sig
    hidden_ref[0] = (act * up_pre).astype(jnp.bfloat16)
    slope = up_pre * sig * (1.0 + gate_pre * (1.0 - sig))
    gate_slope[0] = slope.astype(jnp.bfloat16)
    act_ref[0] = act.astype(jnp.bfloat16)


def backward_kernel(*refs):
    tokens, upstream, ins, outs = refs[:8], refs[8:16], refs[16:21], refs[21:25]
    w_down, hidden, gate_slope, act, gate_rows = ins
    grads, d_gate_out, d_up_out, gate_out = outs
    x, c, c_sems, x_sems, in_sems, out_sems = refs[25:31]
    w_v, hidden_v, slope_v, act_v, rows_v = refs[31:36]
    grads_v, d_gate_v, d_up_v, gate_v = refs[36:40]
    n = w_v.shape[0]
    shards, _, block, ff = grads_v.shape

    def inputs(e):
        pairs = ((w_down, w_v), (hidden, hidden_v), (gate_slope, slope_v), (act, act_v))
        pairs = pairs + ((gate_rows, rows_v),)
        return [
            pltpu.make_async_copy(source.at[e], target.at[e], in_sems.at[e, i])
            for i, (source, target) in enumerate(pairs)
        ]

    def outputs(e):
        pairs = [(grads_v.at[:, 3 * e + m], grads.at[:, 3 * e + m]) for m in range(3)]
        pairs += [
            (d_gate_v.at[e], d_gate_out.at[e]),
            (d_up_v.at[e], d_up_out.at[e]),
            (gate_v.at[e], gate_out.at[e]),
        ]
        return [
            pltpu.make_async_copy(source, target, out_sems.at[e, i])
            for i, (source, target) in enumerate(pairs)
        ]

    def begin(e):
        copies = inputs(e)
        copies[0].start()
        for copy in row_copies(upstream, c, c_sems, e):
            copy.start()
        for copy in copies[1:]:
            copy.start()

    begin(0)
    for e in range(n):
        copies = inputs(e)
        done = outputs(e)
        copies[0].wait()
        for copy in row_copies(upstream, c, c_sems, e):
            copy.wait()
        for copy in row_copies(tokens, x, x_sems, e):
            copy.start()
        here = c[e]
        here = here.reshape(-1, here.shape[-1])
        back = nt(here, w_v[e])
        for copy in copies[1:]:
            copy.wait()
        saved = hidden_v[e].astype(jnp.float32)
        lanes = rows_v.shape[2]
        weight = jnp.concatenate([rows_v[e].astype(jnp.float32)] * (ff // lanes), axis=1)
        terms = saved * back
        gate_v[e] = sum(terms[:, i : i + lanes] for i in range(0, ff, lanes))
        back = back * weight
        d_gate = (back * slope_v[e].astype(jnp.float32)).astype(jnp.bfloat16)
        d_up = (back * act_v[e].astype(jnp.float32)).astype(jnp.bfloat16)
        scaled = (saved * weight).astype(jnp.bfloat16)
        d_gate_v[e] = d_gate
        d_up_v[e] = d_up
        for i in (3, 4, 5):
            done[i].start()
        for r in range(shards):
            total = tn(scaled, here[:, r * block : (r + 1) * block]).astype(jnp.bfloat16)
            for half in range(ff // block):
                grads_v[r, 3 * e + 2, :, half * block : (half + 1) * block] = total[
                    half * block : (half + 1) * block
                ]
        for copy in row_copies(tokens, x, x_sems, e):
            copy.wait()
        if e + 1 < n:
            begin(e + 1)
        done[2].start()
        here = x[e]
        here = here.reshape(-1, here.shape[-1])
        for m, slope in ((0, d_gate), (1, d_up)):
            for r in range(shards):
                total = tn(here[:, r * block : (r + 1) * block], slope)
                grads_v[r, 3 * e + m] = total.astype(jnp.bfloat16)
            done[m].start()
    for e in range(n):
        for copy in outputs(e):
            copy.wait()


def input_kernel(*refs):
    d_gate, d_up, w_gate, w_up = refs[:4]
    outs = refs[4:12]
    gate_v, up_v, w_gate_v, w_up_v, out_v, d_sems, w_sems, out_sems = refs[12:]
    n, _, quarter, _ = w_gate_v.shape[1:]

    def weights(q):
        cols = pl.ds(q * quarter, quarter)
        return [
            pltpu.make_async_copy(source.at[:, cols], target.at[q % 2, :, 0], w_sems.at[q, i])
            for i, (source, target) in enumerate(((w_gate, w_gate_v), (w_up, w_up_v)))
        ]

    def results(q):
        return [
            pltpu.make_async_copy(out_v.at[q, i], outs[q + DIMS * i], out_sems.at[q, i])
            for i in range(2)
        ]

    slopes = [
        pltpu.make_async_copy(d_gate, gate_v, d_sems.at[0]),
        pltpu.make_async_copy(d_up, up_v, d_sems.at[1]),
    ]
    for copy in slopes + weights(0) + weights(1):
        copy.start()
    for copy in slopes:
        copy.wait()
    for q in range(DIMS):
        for copy in weights(q):
            copy.wait()
        for e in range(n):
            total = nt(gate_v[e], w_gate_v[q % 2, e, 0]) + nt(up_v[e], w_up_v[q % 2, e, 0])
            total = total.astype(jnp.bfloat16)
            for p in range(16):
                slot = slot_at(p, q)
                out_v[q, 1 - p // 8, p % 8, e] = total[slot * MOST : (slot + 1) * MOST]
        for copy in results(q):
            copy.start()
        if q + 2 < DIMS:
            for copy in weights(q + 2):
                copy.start()
    for q in range(DIMS):
        for copy in results(q):
            copy.wait()


def one(shape):
    zeros = (0,) * (len(shape) - 1)
    return pl.BlockSpec((1,) + tuple(shape[1:]), lambda e: (e,) + zeros)


def params(mib):
    return pltpu.CompilerParams(
        dimension_semantics=("arbitrary",), vmem_limit_bytes=mib * 1024 * 1024
    )


def forward(parts, w_gate, w_up):
    n, width, ff = w_gate.shape
    count = 16 * MOST
    shapes = [
        ((n, count, ff), jnp.bfloat16),
        ((n, count, ff), jnp.bfloat16),
        ((n, count, ff), jnp.bfloat16),
    ]
    return pl.pallas_call(
        forward_kernel,
        grid=(n,),
        in_specs=[pl.BlockSpec(memory_space=pl.ANY)] * 8 + [one(w_gate.shape), one(w_up.shape)],
        out_specs=[one(s) for s, _ in shapes],
        out_shape=[jax.ShapeDtypeStruct(s, t) for s, t in shapes],
        scratch_shapes=[
            pltpu.VMEM((n, 2, 2, 2, 2, MOST, width), jnp.bfloat16),
            pltpu.SemaphoreType.DMA((n, COPIES)),
        ],
        compiler_params=params(48),
        cost_estimate=pl.CostEstimate(
            flops=4 * n * count * width * ff, bytes_accessed=36 << 20, transcendentals=0
        ),
        name="forward",
    )(*parts, w_gate, w_up)


def backward(tokens, upstream, w_down, saved, gate_rows, shards):
    n, ff, width = w_down.shape
    count = gate_rows.shape[1]
    hidden, gate_slope, act = saved
    shapes = [
        ((shards, 3 * n, width // shards, ff), jnp.bfloat16),
        ((n, count, ff), jnp.bfloat16),
        ((n, count, ff), jnp.bfloat16),
        ((n, count, gate_rows.shape[2]), jnp.float32),
    ]
    ins = (w_down, hidden, gate_slope, act, gate_rows)
    rows = pltpu.VMEM((n, 2, 2, 2, 2, MOST, width), jnp.bfloat16)
    return pl.pallas_call(
        backward_kernel,
        in_specs=[pl.BlockSpec(memory_space=pl.ANY)] * 21,
        out_specs=[pl.BlockSpec(memory_space=pl.ANY)] * 4,
        out_shape=[jax.ShapeDtypeStruct(s, t) for s, t in shapes],
        scratch_shapes=[
            rows,
            rows,
            pltpu.SemaphoreType.DMA((n, COPIES)),
            pltpu.SemaphoreType.DMA((n, COPIES)),
            pltpu.SemaphoreType.DMA((n, 5)),
            pltpu.SemaphoreType.DMA((n, 6)),
        ]
        + [pltpu.VMEM(x.shape, x.dtype) for x in ins]
        + [pltpu.VMEM(s, t) for s, t in shapes],
        compiler_params=pltpu.CompilerParams(vmem_limit_bytes=58 << 20),
        cost_estimate=pl.CostEstimate(
            flops=8 * n * count * width * ff, bytes_accessed=50 << 20, transcendentals=0
        ),
        name="backward",
    )(*tokens, *upstream, *ins)


def input_rows(d_gate, d_up, w_gate, w_up):
    n, width, ff = w_gate.shape
    count = d_gate.shape[1]
    quarter = width // DIMS
    shape = (8, n, MOST, quarter)
    weight = pltpu.VMEM((2, n, 1, quarter, ff), jnp.bfloat16)
    out = pl.pallas_call(
        input_kernel,
        in_specs=[pl.BlockSpec(memory_space=pl.ANY)] * 4,
        out_specs=[pl.BlockSpec(memory_space=pl.ANY)] * 8,
        out_shape=[jax.ShapeDtypeStruct(shape, jnp.bfloat16)] * 8,
        scratch_shapes=[
            pltpu.VMEM(d_gate.shape, jnp.bfloat16),
            pltpu.VMEM(d_up.shape, jnp.bfloat16),
            weight,
            weight,
            pltpu.VMEM((DIMS, 2) + shape, jnp.bfloat16),
            pltpu.SemaphoreType.DMA((2,)),
            pltpu.SemaphoreType.DMA((DIMS, 2)),
            pltpu.SemaphoreType.DMA((DIMS, 2)),
        ],
        compiler_params=pltpu.CompilerParams(vmem_limit_bytes=56 << 20),
        cost_estimate=pl.CostEstimate(
            flops=4 * n * count * width * ff, bytes_accessed=24 << 20, transcendentals=0
        ),
        name="input_rows",
    )(d_gate, d_up, w_gate, w_up)
    return out[:DIMS], out[DIMS:]


def per_device(tokens, cotangent, gates, routes, w_gate, w_up, w_down):
    tok, fanout = routes.shape
    me = lax.axis_index("expert")
    cube = jnp.asarray(CUBE, jnp.int32)[me]
    device_of = jnp.asarray(DEVICE, jnp.int32)

    info = jnp.concatenate([gates, routes.astype(jnp.bfloat16)], axis=1).T
    small = jnp.concatenate([info, jnp.zeros((240, tok), jnp.bfloat16)], axis=0)
    small = lax.all_gather(small, "expert", axis=0, tiled=False)[:, :16]
    near = gather_rows(tokens, cotangent, info)
    devices = device_of[cube ^ jnp.arange(16)]
    small = small[devices]
    gates_rel = small[:, :fanout]
    routes_rel = small[:, fanout:].astype(jnp.int32)

    local = jnp.arange(2, dtype=jnp.int32)
    mine = 2 * me + local
    own_hots = one_hots(routes_rel, mine)
    chosen = routes_rel[:, None] == mine[None, :, None, None]
    gate_tok = jnp.sum(jnp.where(chosen, gates_rel[:, None].astype(jnp.float32), 0.0), axis=2)
    gate_rows = jnp.einsum(
        "jert,jet->ejr",
        own_hots,
        gate_tok.astype(jnp.bfloat16),
        preferred_element_type=jnp.float32,
    ).reshape(2, -1, 1)
    gate_rows = jnp.broadcast_to(gate_rows.astype(jnp.bfloat16), gate_rows.shape[:2] + (tok,))

    picked = [dispatch(q, devices, *near[q]) for q in range(DIMS)]
    firsts = [swap(picked[q][0], (q + 3) % DIMS) for q in range(DIMS)]
    seconds = [swap(picked[q][1], (q + 3) % DIMS) for q in range(DIMS)]
    token_parts = [by_bits(x) for x in [d[2] for d in picked] + firsts]
    upstream_parts = [by_bits(x) for x in [d[3] for d in picked] + seconds]
    hots = [d[4] for d in picked]
    saved = forward(token_parts, w_gate, w_up)
    shards = lax.axis_size("replica")
    grads, d_gate, d_up, gate_grads = backward(
        token_parts, upstream_parts, w_down, saved, gate_rows, shards
    )
    totals = lax.psum_scatter(grads, "replica", scatter_dimension=0, tiled=False)

    fars, rows = input_rows(d_gate, d_up, w_gate, w_up)
    fars, gate_grads = lax.optimization_barrier((fars, gate_grads))

    gate_back = jnp.einsum(
        "jert,ejr->jet",
        own_hots,
        jnp.sum(gate_grads, axis=2).reshape(2, 16, MOST).astype(jnp.bfloat16),
        preferred_element_type=jnp.float32,
    ).astype(jnp.bfloat16)
    gate_back = gate_back[cube ^ jnp.asarray(CUBE, jnp.int32)]
    gate_back = lax.all_to_all(gate_back, "expert", split_axis=0, concat_axis=0, tiled=True)
    gots = [swap(fars[q], (q + 3) % DIMS) for q in range(DIMS)]
    gots[1:], gate_back = lax.optimization_barrier((gots[1:], gate_back))
    by_expert = gate_back.reshape(32, tok)
    chosen = routes[:, None, :] == jnp.arange(32, dtype=jnp.int32)[None, :, None]
    grad_gates = jnp.sum(
        jnp.where(chosen, by_expert.T[:, :, None].astype(jnp.float32), 0.0), axis=1
    ).astype(jnp.bfloat16)

    parts = []
    for q in range(DIMS):
        keep, send = combine(hots[q], rows[q], gots[q])
        for s in (2, 1, 0):
            got = swap(send, (q + s) % DIMS)
            half = keep.shape[0] // 2
            if s:
                send = (keep[half:].astype(jnp.float32) + got[half:].astype(jnp.float32)).astype(
                    jnp.bfloat16
                )
                keep, got = keep[:half], got[:half]
            keep = (keep.astype(jnp.float32) + got.astype(jnp.float32)).astype(jnp.bfloat16)
        parts.append(keep[0])
    grad_input = jnp.concatenate(parts, axis=1)
    down = totals[2::3]
    block = down.shape[1]
    down = jnp.concatenate(
        [down[:, :, block * half : block * (half + 1)] for half in range(down.shape[2] // block)],
        axis=1,
    )
    return grad_input, grad_gates, totals[0::3], totals[1::3], down


def solution(mesh):
    tok = P(("expert", "replica"), None)
    return jax.shard_map(
        per_device,
        mesh=mesh,
        in_specs=(tok, tok, tok, tok) + (P("expert", None, None),) * 3,
        out_specs=(
            tok,
            tok,
            P("expert", "replica", None),
            P("expert", "replica", None),
            P("expert", None, "replica"),
        ),
        check_vma=False,
    )
```

```python
import jax
import jax.numpy as jnp
from jax import lax
from jax.experimental import pallas as pl
from jax.experimental.pallas import tpu as pltpu
from jax.sharding import PartitionSpec as P

MOST = 48
SIDE = 4
DIMS = 4
GRAY = (0, 1, 3, 2)


def flip(axis, bit):
    other = (1, 0, 3, 2) if bit == 0 else (3, 2, 1, 0)
    pairs = []
    for y in range(SIDE):
        for x in range(SIDE):
            ny, nx = (y, other[x]) if axis == "x" else (other[y], x)
            pairs.append((y * SIDE + x, ny * SIDE + nx))
    return pairs


PERMS = (flip("x", 0), flip("y", 0), flip("x", 1), flip("y", 1))


def cube_of(device):
    gx, gy = GRAY[device % SIDE], GRAY[device // SIDE]
    return (gx & 1) | ((gy & 1) << 1) | ((gx >> 1) << 2) | ((gy >> 1) << 3)


CUBE = [cube_of(d) for d in range(16)]
DEVICE = [CUBE.index(c) for c in range(16)]


def slot_at(position, quarter):
    return sum(((position >> s) & 1) << ((quarter + s) % DIMS) for s in range(DIMS))


def swap(x, dim):
    return lax.ppermute(x, "expert", PERMS[dim])


def one_hots(routes_rel, expert_ids):
    hit = jnp.any(routes_rel[:, None] == expert_ids[None, :, None, None], axis=2)
    tok = routes_rel.shape[2]
    before = jnp.arange(tok)[:, None] < jnp.arange(tok)[None, :]
    rank = jnp.einsum(
        "net,tu->neu",
        hit.astype(jnp.bfloat16),
        before.astype(jnp.bfloat16),
        preferred_element_type=jnp.float32,
    )
    at = jnp.where(hit, rank, -1.0)
    rows = jnp.arange(MOST, dtype=jnp.float32)
    return (at[:, :, None, :] == rows[None, None, :, None]).astype(jnp.bfloat16)


EXTRA = 16


def gather_rows(tokens, cotangent, small):
    width = tokens.shape[1] // DIMS
    small = small.reshape(-1, width)
    small = jnp.concatenate([small, jnp.zeros((EXTRA - small.shape[0], width), small.dtype)])
    near = []
    for q in range(DIMS):
        cols = slice(width * q, width * (q + 1))
        near.append(jnp.concatenate([tokens[:, cols], cotangent[:, cols], small])[None])
    for s in range(DIMS - 1):
        got = [swap(near[q], (q + s) % DIMS) for q in range(DIMS)]
        if s == DIMS - 2:
            return list(zip(near, got))
        near = [jnp.concatenate([a, b], axis=0) for a, b in zip(near, got)]


def dispatch_kernel(q, device_ref, low, high, send_a, send_b, own_a, own_b, hots):
    count, rows, width = low.shape
    tok = (rows - EXTRA) // 2
    per_row = width // tok
    here = device_ref[0]
    partner = device_ref[1 << ((q + 3) % DIMS)]
    lower = lax.broadcasted_iota(jnp.int32, (tok, tok), 0)
    before = (lower < lax.broadcasted_iota(jnp.int32, (tok, tok), 1)).astype(jnp.bfloat16)
    index = lax.broadcasted_iota(jnp.int32, (MOST, tok), 0).astype(jnp.float32)

    def half(near):
        hits = []
        for p in range(count):
            small = near[p, 2 * tok :, :].astype(jnp.float32)
            routes = jnp.concatenate(
                [
                    small[i // per_row : i // per_row + 1, i % per_row * tok : (i % per_row + 1) * tok]
                    for i in range(8, 16)
                ],
                axis=0,
            )
            for target in (here, partner):
                for local in range(2):
                    expert = (2 * target + local).astype(jnp.float32)
                    same = (routes == expert).astype(jnp.float32)
                    hits.append(jnp.max(same, axis=0, keepdims=True))
        hit = jnp.concatenate(hits, axis=0)
        rank = jnp.dot(hit.astype(jnp.bfloat16), before, preferred_element_type=jnp.float32)
        at = jnp.where(hit > 0.0, rank, -1.0)
        for p in range(count):
            hot = jnp.concatenate(
                [(index == at[4 * p + i : 4 * p + i + 1]).astype(jnp.bfloat16) for i in range(4)],
                axis=0,
            )
            hots[p] = hot
            none = jnp.zeros_like(hot)
            both = jnp.concatenate(
                [
                    jnp.concatenate([hot, none], axis=1),
                    jnp.concatenate([none, hot], axis=1),
                ],
                axis=0,
            )
            out = jnp.dot(both, near[p, : 2 * tok], preferred_element_type=jnp.float32)
            out = out.astype(jnp.bfloat16)
            for i, rows_out in enumerate((own_a, send_a, own_b, send_b)):
                for local in range(2):
                    at_row = (2 * i + local) * MOST
                    rows_out[p, local] = out[at_row : at_row + MOST]

    @pl.when(pl.program_id(0) == 0)
    def _():
        half(low)

    @pl.when(pl.program_id(0) == 1)
    def _():
        half(high)


def dispatch(q, devices, low, high):
    block, length, width = low.shape
    tok = (length - EXTRA) // 2
    count = 2 * block
    rows = (count, 2, MOST, width)
    row_block = pl.BlockSpec((block,) + rows[1:], lambda i, d: (i, 0, 0, 0))
    whole = pl.BlockSpec(low.shape, lambda i, d: (0, 0, 0))

    def kernel(*refs):
        dispatch_kernel(q, *refs)

    return pl.pallas_call(
        kernel,
        grid_spec=pltpu.PrefetchScalarGridSpec(
            num_scalar_prefetch=1,
            grid=(2,),
            in_specs=[whole, whole],
            out_specs=[row_block] * 4
            + [pl.BlockSpec((block, 4 * MOST, tok), lambda i, d: (i, 0, 0))],
        ),
        out_shape=[jax.ShapeDtypeStruct(rows, jnp.bfloat16)] * 4
        + [jax.ShapeDtypeStruct((count, 4 * MOST, tok), jnp.bfloat16)],
        compiler_params=params(58),
        cost_estimate=pl.CostEstimate(
            flops=2 * count * 2 * 4 * MOST * tok * width,
            bytes_accessed=6 << 20,
            transcendentals=0,
        ),
        name="dispatch",
    )(devices, low, high)


def combine_kernel(hots, own, got, keep, send):
    count = own.shape[0]

    def fill(out):
        for p in range(count):
            rows = jnp.concatenate([own[p, 0], own[p, 1], got[p, 0], got[p, 1]], axis=0)
            out[p] = lax.dot_general(
                hots[p], rows, (((0,), (0,)), ((), ())), preferred_element_type=jnp.float32
            ).astype(jnp.bfloat16)

    @pl.when(pl.program_id(0) == 0)
    def _():
        fill(send)

    @pl.when(pl.program_id(0) == 1)
    def _():
        fill(keep)


def combine(hots, own, got):
    count, _, _, width = own.shape
    tok = hots.shape[2]
    block = count // 2
    row_block = pl.BlockSpec((block,) + own.shape[1:], lambda i: (1 - i, 0, 0, 0))
    out = pl.BlockSpec((block, tok, width), lambda i: (0, 0, 0))
    return pl.pallas_call(
        combine_kernel,
        grid=(2,),
        in_specs=[
            pl.BlockSpec((block,) + hots.shape[1:], lambda i: (1 - i, 0, 0)),
            row_block,
            row_block,
        ],
        out_specs=[out, out],
        out_shape=[jax.ShapeDtypeStruct((block, tok, width), jnp.bfloat16)] * 2,
        compiler_params=params(24),
        cost_estimate=pl.CostEstimate(
            flops=2 * count * 4 * MOST * tok * width, bytes_accessed=4 << 20, transcendentals=0
        ),
        name="combine",
    )(hots, own, got)


def by_bits(rows):
    return rows.reshape((2, 2, 2) + rows.shape[1:])


def row_copies(parts, rows, sems, e):
    copies = []
    for q in range(DIMS):
        for bit in range(2):
            part = parts[q + DIMS * bit]
            width = part.shape[-1]
            cols = pl.ds(q * width, width)
            if q == 0:
                pairs = [(part.at[:, :, :, e], rows.at[e, bit, :, :, :, :, cols])]
            elif q == 1:
                pairs = [(part.at[:, :, :, e], rows.at[e, :, :, :, bit, :, cols])]
            elif q == 2:
                pairs = [
                    (part.at[low, :, :, e], rows.at[e, :, :, bit, low, :, cols])
                    for low in range(2)
                ]
            else:
                pairs = [
                    (part.at[mid, low, :, e], rows.at[e, :, bit, mid, low, :, cols])
                    for mid in range(2)
                    for low in range(2)
                ]
            for source, target in pairs:
                copies.append(pltpu.make_async_copy(source, target, sems.at[e, len(copies)]))
    return copies


COPIES = 16


def load_rows(parts, rows, sems):
    e = pl.program_id(0)

    @pl.when(e == 0)
    def _():
        for which in range(2):
            for copy in row_copies(parts, rows, sems, which):
                copy.start()

    for which in range(2):

        @pl.when(e == which)
        def _():
            for copy in row_copies(parts, rows, sems, which):
                copy.wait()

    here = rows[e]
    return here.reshape(-1, here.shape[-1])


def nt(a, b):
    return lax.dot_general(a, b, (((1,), (1,)), ((), ())), preferred_element_type=jnp.float32)


def nn(a, b):
    return jnp.dot(a, b, preferred_element_type=jnp.float32)


def tn(a, b):
    return lax.dot_general(a, b, (((0,), (0,)), ((), ())), preferred_element_type=jnp.float32)


def forward_kernel(*refs):
    parts, (w_gate, w_up), outs = refs[:8], refs[8:10], refs[10:13]
    rows, sems = refs[13:]
    hidden_ref, gate_slope, act_ref = outs
    here = load_rows(parts, rows, sems)
    gate_pre = nn(here, w_gate[0])
    up_pre = nn(here, w_up[0])
    sig = jax.nn.sigmoid(gate_pre)
    act = gate_pre * sig
    hidden_ref[0] = (act * up_pre).astype(jnp.bfloat16)
    slope = up_pre * sig * (1.0 + gate_pre * (1.0 - sig))
    gate_slope[0] = slope.astype(jnp.bfloat16)
    act_ref[0] = act.astype(jnp.bfloat16)


def backward_kernel(*refs):
    tokens, upstream, ins, outs = refs[:8], refs[8:16], refs[16:21], refs[21:25]
    w_down, hidden, gate_slope, act, gate_rows = ins
    grads, d_gate_out, d_up_out, gate_out = outs
    x, c, c_sems, x_sems, in_sems, out_sems = refs[25:31]
    w_v, hidden_v, slope_v, act_v, rows_v = refs[31:36]
    grads_v, d_gate_v, d_up_v, gate_v = refs[36:40]
    n = w_v.shape[0]
    shards, _, block, ff = grads_v.shape

    def inputs(e):
        pairs = ((w_down, w_v), (hidden, hidden_v), (gate_slope, slope_v), (act, act_v))
        pairs = pairs + ((gate_rows, rows_v),)
        return [
            pltpu.make_async_copy(source.at[e], target.at[e], in_sems.at[e, i])
            for i, (source, target) in enumerate(pairs)
        ]

    def outputs(e):
        pairs = [(grads_v.at[:, 3 * e + m], grads.at[:, 3 * e + m]) for m in range(3)]
        pairs += [
            (d_gate_v.at[e], d_gate_out.at[e]),
            (d_up_v.at[e], d_up_out.at[e]),
            (gate_v.at[e], gate_out.at[e]),
        ]
        return [
            pltpu.make_async_copy(source, target, out_sems.at[e, i])
            for i, (source, target) in enumerate(pairs)
        ]

    def columns(ref, e, r):
        part = ref[e, :, :, :, :, :, pl.ds(pl.multiple_of(r * block, block), block)]
        return part.reshape(-1, block)

    def begin(e):
        copies = inputs(e)
        copies[0].start()
        for copy in row_copies(upstream, c, c_sems, e):
            copy.start()
        for copy in copies[1:]:
            copy.start()

    begin(0)
    for e in range(n):
        copies = inputs(e)
        done = outputs(e)
        copies[0].wait()
        for copy in row_copies(upstream, c, c_sems, e):
            copy.wait()
        for copy in row_copies(tokens, x, x_sems, e):
            copy.start()
        here = c[e]
        here = here.reshape(-1, here.shape[-1])
        back = nt(here, w_v[e])
        for copy in copies[1:]:
            copy.wait()
        saved = hidden_v[e].astype(jnp.float32)
        lanes = rows_v.shape[2]
        weight = jnp.concatenate([rows_v[e].astype(jnp.float32)] * (ff // lanes), axis=1)
        terms = saved * back
        gate_v[e] = sum(terms[:, i : i + lanes] for i in range(0, ff, lanes))
        back = back * weight
        d_gate = (back * slope_v[e].astype(jnp.float32)).astype(jnp.bfloat16)
        d_up = (back * act_v[e].astype(jnp.float32)).astype(jnp.bfloat16)
        scaled = (saved * weight).astype(jnp.bfloat16)
        d_gate_v[e] = d_gate
        d_up_v[e] = d_up
        for i in (3, 4, 5):
            done[i].start()

        @pl.loop(0, shards)
        def _(r):
            total = tn(scaled, columns(c, e, r)).astype(jnp.bfloat16)
            for half in range(ff // block):
                grads_v[r, 3 * e + 2, :, half * block : (half + 1) * block] = total[
                    half * block : (half + 1) * block
                ]
        for copy in row_copies(tokens, x, x_sems, e):
            copy.wait()
        if e + 1 < n:
            begin(e + 1)
        done[2].start()
        for m, slope in ((0, d_gate), (1, d_up)):

            @pl.loop(0, shards)
            def _(r):
                grads_v[r, 3 * e + m] = tn(columns(x, e, r), slope).astype(jnp.bfloat16)

            done[m].start()
    for e in range(n):
        for copy in outputs(e):
            copy.wait()


def input_kernel(*refs):
    d_gate, d_up, w_gate, w_up = refs[:4]
    outs = refs[4:12]
    gate_v, up_v, w_gate_v, w_up_v, out_v, d_sems, w_sems, out_sems = refs[12:]
    n, _, quarter, _ = w_gate_v.shape[1:]

    def weights(q):
        cols = pl.ds(q * quarter, quarter)
        return [
            pltpu.make_async_copy(source.at[:, cols], target.at[q % 2, :, 0], w_sems.at[q, i])
            for i, (source, target) in enumerate(((w_gate, w_gate_v), (w_up, w_up_v)))
        ]

    def results(q):
        return [
            pltpu.make_async_copy(out_v.at[q, i], outs[q + DIMS * i], out_sems.at[q, i])
            for i in range(2)
        ]

    slopes = [
        pltpu.make_async_copy(d_gate, gate_v, d_sems.at[0]),
        pltpu.make_async_copy(d_up, up_v, d_sems.at[1]),
    ]
    for copy in slopes + weights(0) + weights(1):
        copy.start()
    for copy in slopes:
        copy.wait()
    for q in range(DIMS):
        for copy in weights(q):
            copy.wait()
        for e in range(n):
            total = nt(gate_v[e], w_gate_v[q % 2, e, 0]) + nt(up_v[e], w_up_v[q % 2, e, 0])
            total = total.astype(jnp.bfloat16)
            for p in range(16):
                slot = slot_at(p, q)
                out_v[q, 1 - p // 8, p % 8, e] = total[slot * MOST : (slot + 1) * MOST]
        for copy in results(q):
            copy.start()
        if q + 2 < DIMS:
            for copy in weights(q + 2):
                copy.start()
    for q in range(DIMS):
        for copy in results(q):
            copy.wait()


def one(shape):
    zeros = (0,) * (len(shape) - 1)
    return pl.BlockSpec((1,) + tuple(shape[1:]), lambda e: (e,) + zeros)


def params(mib):
    return pltpu.CompilerParams(
        dimension_semantics=("arbitrary",), vmem_limit_bytes=mib * 1024 * 1024
    )


def forward(parts, w_gate, w_up):
    n, width, ff = w_gate.shape
    count = 16 * MOST
    shapes = [
        ((n, count, ff), jnp.bfloat16),
        ((n, count, ff), jnp.bfloat16),
        ((n, count, ff), jnp.bfloat16),
    ]
    return pl.pallas_call(
        forward_kernel,
        grid=(n,),
        in_specs=[pl.BlockSpec(memory_space=pl.ANY)] * 8 + [one(w_gate.shape), one(w_up.shape)],
        out_specs=[one(s) for s, _ in shapes],
        out_shape=[jax.ShapeDtypeStruct(s, t) for s, t in shapes],
        scratch_shapes=[
            pltpu.VMEM((n, 2, 2, 2, 2, MOST, width), jnp.bfloat16),
            pltpu.SemaphoreType.DMA((n, COPIES)),
        ],
        compiler_params=params(48),
        cost_estimate=pl.CostEstimate(
            flops=4 * n * count * width * ff, bytes_accessed=36 << 20, transcendentals=0
        ),
        name="forward",
    )(*parts, w_gate, w_up)


def backward(tokens, upstream, w_down, saved, gate_rows, shards):
    n, ff, width = w_down.shape
    count = gate_rows.shape[1]
    hidden, gate_slope, act = saved
    shapes = [
        ((shards, 3 * n, width // shards, ff), jnp.bfloat16),
        ((n, count, ff), jnp.bfloat16),
        ((n, count, ff), jnp.bfloat16),
        ((n, count, gate_rows.shape[2]), jnp.float32),
    ]
    ins = (w_down, hidden, gate_slope, act, gate_rows)
    rows = pltpu.VMEM((n, 2, 2, 2, 2, MOST, width), jnp.bfloat16)
    return pl.pallas_call(
        backward_kernel,
        in_specs=[pl.BlockSpec(memory_space=pl.ANY)] * 21,
        out_specs=[pl.BlockSpec(memory_space=pl.ANY)] * 4,
        out_shape=[jax.ShapeDtypeStruct(s, t) for s, t in shapes],
        scratch_shapes=[
            rows,
            rows,
            pltpu.SemaphoreType.DMA((n, COPIES)),
            pltpu.SemaphoreType.DMA((n, COPIES)),
            pltpu.SemaphoreType.DMA((n, 5)),
            pltpu.SemaphoreType.DMA((n, 6)),
        ]
        + [pltpu.VMEM(x.shape, x.dtype) for x in ins]
        + [pltpu.VMEM(s, t) for s, t in shapes],
        compiler_params=pltpu.CompilerParams(vmem_limit_bytes=58 << 20),
        cost_estimate=pl.CostEstimate(
            flops=8 * n * count * width * ff, bytes_accessed=50 << 20, transcendentals=0
        ),
        name="backward",
    )(*tokens, *upstream, *ins)


def input_rows(d_gate, d_up, w_gate, w_up):
    n, width, ff = w_gate.shape
    count = d_gate.shape[1]
    quarter = width // DIMS
    shape = (8, n, MOST, quarter)
    weight = pltpu.VMEM((2, n, 1, quarter, ff), jnp.bfloat16)
    out = pl.pallas_call(
        input_kernel,
        in_specs=[pl.BlockSpec(memory_space=pl.ANY)] * 4,
        out_specs=[pl.BlockSpec(memory_space=pl.ANY)] * 8,
        out_shape=[jax.ShapeDtypeStruct(shape, jnp.bfloat16)] * 8,
        scratch_shapes=[
            pltpu.VMEM(d_gate.shape, jnp.bfloat16),
            pltpu.VMEM(d_up.shape, jnp.bfloat16),
            weight,
            weight,
            pltpu.VMEM((DIMS, 2) + shape, jnp.bfloat16),
            pltpu.SemaphoreType.DMA((2,)),
            pltpu.SemaphoreType.DMA((DIMS, 2)),
            pltpu.SemaphoreType.DMA((DIMS, 2)),
        ],
        compiler_params=pltpu.CompilerParams(vmem_limit_bytes=56 << 20),
        cost_estimate=pl.CostEstimate(
            flops=4 * n * count * width * ff, bytes_accessed=24 << 20, transcendentals=0
        ),
        name="input_rows",
    )(d_gate, d_up, w_gate, w_up)
    return out[:DIMS], out[DIMS:]


def per_device(tokens, cotangent, gates, routes, w_gate, w_up, w_down):
    tok, fanout = routes.shape
    me = lax.axis_index("expert")
    cube = jnp.asarray(CUBE, jnp.int32)[me]
    device_of = jnp.asarray(DEVICE, jnp.int32)

    info = jnp.concatenate([gates, routes.astype(jnp.bfloat16)], axis=1).T
    small = jnp.concatenate([info, jnp.zeros((240, tok), jnp.bfloat16)], axis=0)
    small = lax.all_gather(small, "expert", axis=0, tiled=False)[:, :16]
    near = gather_rows(tokens, cotangent, info)
    devices = device_of[cube ^ jnp.arange(16)]
    small = small[devices]
    gates_rel = small[:, :fanout]
    routes_rel = small[:, fanout:].astype(jnp.int32)

    local = jnp.arange(2, dtype=jnp.int32)
    mine = 2 * me + local
    own_hots = one_hots(routes_rel, mine)
    chosen = routes_rel[:, None] == mine[None, :, None, None]
    gate_tok = jnp.sum(jnp.where(chosen, gates_rel[:, None].astype(jnp.float32), 0.0), axis=2)
    gate_rows = jnp.einsum(
        "jert,jet->ejr",
        own_hots,
        gate_tok.astype(jnp.bfloat16),
        preferred_element_type=jnp.float32,
    ).reshape(2, -1, 1)
    gate_rows = jnp.broadcast_to(gate_rows.astype(jnp.bfloat16), gate_rows.shape[:2] + (tok,))

    picked = [dispatch(q, devices, *near[q]) for q in range(DIMS)]
    firsts = [swap(picked[q][0], (q + 3) % DIMS) for q in range(DIMS)]
    seconds = [swap(picked[q][1], (q + 3) % DIMS) for q in range(DIMS)]
    token_parts = [by_bits(x) for x in [d[2] for d in picked] + firsts]
    upstream_parts = [by_bits(x) for x in [d[3] for d in picked] + seconds]
    hots = [d[4] for d in picked]
    saved = forward(token_parts, w_gate, w_up)
    shards = lax.axis_size("replica")
    grads, d_gate, d_up, gate_grads = backward(
        token_parts, upstream_parts, w_down, saved, gate_rows, shards
    )
    totals = lax.psum_scatter(grads, "replica", scatter_dimension=0, tiled=False)

    fars, rows = input_rows(d_gate, d_up, w_gate, w_up)
    fars, gate_grads = lax.optimization_barrier((fars, gate_grads))

    gate_back = jnp.einsum(
        "jert,ejr->jet",
        own_hots,
        jnp.sum(gate_grads, axis=2).reshape(2, 16, MOST).astype(jnp.bfloat16),
        preferred_element_type=jnp.float32,
    ).astype(jnp.bfloat16)
    gate_back = gate_back[cube ^ jnp.asarray(CUBE, jnp.int32)]
    gate_back = lax.all_to_all(gate_back, "expert", split_axis=0, concat_axis=0, tiled=True)
    gots = [swap(fars[q], (q + 3) % DIMS) for q in range(DIMS)]
    gots[1:], gate_back = lax.optimization_barrier((gots[1:], gate_back))
    by_expert = gate_back.reshape(32, tok)
    chosen = routes[:, None, :] == jnp.arange(32, dtype=jnp.int32)[None, :, None]
    grad_gates = jnp.sum(
        jnp.where(chosen, by_expert.T[:, :, None].astype(jnp.float32), 0.0), axis=1
    ).astype(jnp.bfloat16)

    parts = []
    for q in range(DIMS):
        keep, send = combine(hots[q], rows[q], gots[q])
        for s in (2, 1, 0):
            got = swap(send, (q + s) % DIMS)
            half = keep.shape[0] // 2
            if s:
                send = (keep[half:].astype(jnp.float32) + got[half:].astype(jnp.float32)).astype(
                    jnp.bfloat16
                )
                keep, got = keep[:half], got[:half]
            keep = (keep.astype(jnp.float32) + got.astype(jnp.float32)).astype(jnp.bfloat16)
        parts.append(keep[0])
    grad_input = jnp.concatenate(parts, axis=1)
    down = totals[2::3]
    block = down.shape[1]
    down = jnp.concatenate(
        [down[:, :, block * half : block * (half + 1)] for half in range(down.shape[2] // block)],
        axis=1,
    )
    return grad_input, grad_gates, totals[0::3], totals[1::3], down


def solution(mesh):
    tok = P(("expert", "replica"), None)
    return jax.shard_map(
        per_device,
        mesh=mesh,
        in_specs=(tok, tok, tok, tok) + (P("expert", None, None),) * 3,
        out_specs=(
            tok,
            tok,
            P("expert", "replica", None),
            P("expert", "replica", None),
            P("expert", None, "replica"),
        ),
        check_vma=False,
    )
```
